32 devices in a mesh: groups: 2 (over y), dom: 4 (over z), rep: 4 (over x, core).
Axes of the slice: x: 2, y: 2, z: 4, core: 2. Of those that a mesh axis runs over, the one named last changes fastest.
Arguments:
- grad_out: bfloat16 [8192, 512], P(('groups', 'dom')), parts along dimension 0, may hold values from -6 to 6
- source_features: bfloat16 [16384, 512], P(('groups', 'dom')), parts along dimension 0, may hold values from -6 to 6
- rel_weight: bfloat16 [8, 512, 512], P('rep'), may hold values from -0.25 to 0.25
- self_weight: bfloat16 [512, 512], P('rep'), may hold values from -0.25 to 0.25
- edge_dst: int32 [8, 32768], P('rep', ('groups', 'dom')), parts along dimension 1, may hold values from 0 to 1023
- edge_src: int32 [8, 32768], P('rep', ('groups', 'dom')), parts along dimension 1, may hold values from 0 to 2047
- send_counts: int32 [8, 4], P(('groups', 'dom')), parts along dimension 0, may hold values from 1 to 512, as said below
- target_rows: int32 [32, 512], P(('groups', 'dom')), parts along dimension 0, may hold values from 0 to 2047
Outputs:
- grad_owned: float32 [16384, 512], P(('groups', 'dom'), 'rep'), parts along dimension 0
- grad_rel_weight: float32 [16, 512, 512], P(('groups', 'rep')), parts along dimension 0
The draws below stay inside these ranges and needn't reach their ends.
There are 2 independent parts, one for each index of `groups`. The reference program is written for one: setup_inputs(seed, part) draws one part's arguments, and reference() takes and returns one part's arrays. A program takes and returns all parts, laid end to end along the dimension named above; an argument that names none is the same for every part. Nothing has to cross between parts.
Inputs may be any that keep to these rules, and one draw needn't show every extreme that they name: `send_counts`: each device has some owner to which all 512 of its slots are used.
All inputs are finite; a program needn't handle non-finite values.
Results may differ from the reference program's by a relative error of at most 0.0034.
Values sent between devices are 32-bit elements; how exact they have to be, the bound alone decides.
A program may use at most 128 MiB of HBM per device.

```python
import jax
import jax.numpy as jnp
from jax import lax

H = 512
R = 8
DST_DEV = 1024
SRC_DEV = 2048
OWN_DEV = 2048
EDGE_DEV = 4096
SLOT = 512
DST = 4096
SRC = 8192
EDGES = 16384
PAIRS = 16
N_DOM = 4


def draw_send_counts(key, part):
    key = jax.random.fold_in(key, 11)
    first, second, third = jax.random.split(key, 3)
    base = jax.random.randint(first, (N_DOM, N_DOM), 1, SLOT + 1)
    factor = jax.random.randint(second, (1, N_DOM), 1, 5)
    counts = jnp.maximum(1, base * factor // 4)
    offset = jax.random.randint(third, (N_DOM, 1), 0, N_DOM)
    columns = jnp.arange(N_DOM)[None, :]
    full = columns == (jnp.arange(N_DOM)[:, None] + offset) % N_DOM
    return jnp.where(full, SLOT, counts).astype(jnp.int32)


def set_ends(drawn, key, least, top_value):
    spot = [jax.random.randint(jax.random.fold_in(key, axis), (), 0, length) for axis, length in enumerate(drawn.shape)]
    longest = drawn.shape.index(max(drawn.shape))
    neighbour = spot[:longest] + [(spot[longest] + 1) % drawn.shape[longest]] + spot[longest + 1:]
    return drawn.at[tuple(spot)].set(least).at[tuple(neighbour)].set(top_value)


def levels(own_key, dims, shards, least, high):
    loudness, own = 1.0, jax.random.fold_in(own_key, 6)
    for axis_at, parts in shards:
        heights = jnp.exp(jax.random.uniform(jax.random.fold_in(own, axis_at), (parts,), jnp.float32, least / len(shards), high / len(shards)))
        loudness = loudness * jnp.repeat(heights, dims[axis_at] // parts).reshape([-1 if axis == axis_at else 1 for axis in range(len(dims))])
    return loudness


def noise(rng, dims, spread, reach, pieces=(), kind=jnp.bfloat16):
    drawn = jax.random.normal(rng, dims, jnp.float32) * spread
    if len(pieces) > 0:
        drawn = levels(rng, dims, pieces, -0.22, 0.18) * drawn
    return jnp.clip(drawn, min=-reach, max=reach).astype(kind)


def setup_inputs(seed: int = 0, part: int = 0) -> dict:
    seeds = jax.random.split(jax.random.key(seed), 9)
    part_keys = jax.random.split(jax.random.fold_in(seeds[8], part), 9)
    grad_out = noise(part_keys[0], (DST, H), 1.0, 6.0, ((0, 4),))
    source_features = noise(part_keys[1], (SRC, H), 1.0, 6.0, ((0, 4),))
    rel_weight = noise(seeds[2], (R, H, H), H ** -0.5, 0.25, ((0, 4),))
    self_weight = noise(seeds[3], (H, H), H ** -0.5, 0.25, ((0, 4),))
    edge_dst = set_ends(jax.random.randint(part_keys[4], (R, EDGES), 0, DST_DEV), jax.random.fold_in(part_keys[4], 1), 0, DST_DEV - 1).astype(jnp.int32)
    edge_src = set_ends(jax.random.randint(part_keys[5], (R, EDGES), 0, SRC_DEV), jax.random.fold_in(part_keys[5], 1), 0, SRC_DEV - 1).astype(jnp.int32)
    send_counts = draw_send_counts(jax.random.fold_in(jax.random.fold_in(seeds[8], part), 71), part)
    target_rows = set_ends(jax.random.randint(part_keys[7], (PAIRS, SLOT), 0, OWN_DEV), jax.random.fold_in(part_keys[7], 1), 0, OWN_DEV - 1).astype(jnp.int32)
    return dict(grad_out=grad_out, source_features=source_features, rel_weight=rel_weight, self_weight=self_weight, edge_dst=edge_dst, edge_src=edge_src, send_counts=send_counts, target_rows=target_rows)


def remap_slots(src, counts, slot_index):
    block = src // slot_index
    pos = src % slot_index
    return (block * slot_index + pos % counts[block]).astype(jnp.int32)


def device_terms(grad_rows, feats, weights, dst, src, counts):
    slot_index = feats.shape[0] // counts.shape[0]
    width = grad_rows.shape[1]

    def one(dst_r, src_r):
        fixed_portion = remap_slots(src_r, counts, slot_index)
        degree = jnp.zeros((grad_rows.shape[0],), jnp.float32).at[dst_r].add(1.0)
        norm = 1.0 / jnp.maximum(degree, 1.0)
        scaled = (grad_rows.astype(jnp.float32) * norm[:, None]).astype(jnp.bfloat16)
        rows = scaled[dst_r].astype(jnp.float32)
        return jnp.zeros((feats.shape[0], width), jnp.float32).at[fixed_portion].add(rows).astype(jnp.bfloat16)

    pulled = jax.vmap(one)(dst, src)
    pulled32 = pulled.astype(jnp.float32)
    partial_value = jnp.einsum("rso,rio->si", pulled32, weights.astype(jnp.float32))
    wgrad = jnp.einsum("si,rso->rio", feats.astype(jnp.float32), pulled32)
    return partial_value, wgrad


def reference(grad_out, source_features, rel_weight, self_weight, edge_dst, edge_src, send_counts, target_rows):
    ndev = send_counts.shape[0]
    grad_blocks = grad_out.reshape(ndev, DST_DEV, H)
    feat_blocks = source_features.reshape(ndev, SRC_DEV, H)
    dst_blocks = jnp.transpose(edge_dst.reshape(R, ndev, EDGE_DEV), (1, 0, 2))
    src_blocks = jnp.transpose(edge_src.reshape(R, ndev, EDGE_DEV), (1, 0, 2))

    def step(carry, item):
        grad_rows, feats, dst, src, counts = item
        partial_value, wgrad = device_terms(grad_rows, feats, rel_weight, dst, src, counts)
        return carry + wgrad, partial_value

    start = jnp.zeros((R, H, H), jnp.float32)
    grad_rel_weight, partials = lax.scan(step, start, (grad_blocks, feat_blocks, dst_blocks, src_blocks, send_counts))
    slot_index = SRC_DEV // ndev
    routed = jnp.transpose(partials.reshape(ndev, ndev, slot_index, H), (1, 0, 2, 3)).reshape(ndev, ndev * slot_index, H)
    targets = target_rows.reshape(ndev, ndev * slot_index)

    def deliver(rows_at, values):
        return jnp.zeros((OWN_DEV, H), jnp.float32).at[rows_at].add(values)

    owned = jax.vmap(deliver)(targets, routed)
    self_term = jnp.einsum("ndo,io->ndi", grad_blocks.astype(jnp.float32), self_weight.astype(jnp.float32))
    owned = owned.at[:, :DST_DEV].add(self_term)
    return owned.reshape(ndev * OWN_DEV, H), grad_rel_weight
```

```python
import math

import jax
import jax.numpy as jnp
from jax import lax
from jax.sharding import PartitionSpec as P

OWN_DEV = 2048


def remap_slots(source, counts, slot_index, domain_count):
    block = source // slot_index
    position = source % slot_index
    picked = jnp.sum(
        jnp.where(block[:, None] == jnp.arange(domain_count)[None, :], counts[None, :], 0), axis=1
    )
    return block * slot_index + position % picked


def deliver(targets, arrived, owned_rows):
    step_rows = math.gcd(owned_rows, 512)
    starts = jnp.arange(0, owned_rows, step_rows, dtype=jnp.int32)

    def one_block(start):
        wanted = start + jnp.arange(step_rows, dtype=jnp.int32)
        picks = (targets[None, :] == wanted[:, None]).astype(jnp.float32)
        return jnp.dot(
            picks, arrived, precision=lax.Precision.HIGHEST, preferred_element_type=jnp.float32
        )

    blocks = lax.map(one_block, starts)
    return blocks.reshape(owned_rows, arrived.shape[1])


def on_device(
    grad_out, source_features, rel_weight, self_weight, edge_dst, edge_src, send_counts, target_rows
):
    domain_count = lax.axis_size("dom")
    slot_count = source_features.shape[0]
    slot_index = slot_count // domain_count
    destination_count = grad_out.shape[0]
    counts = send_counts[0]

    def one(pair):
        destination_relation, src_rel = pair
        fixed_portion = remap_slots(src_rel, counts, slot_index, domain_count)
        running_tally = (
            jnp.zeros((slot_count, destination_count), jnp.float32)
            .at[fixed_portion, destination_relation]
            .add(1.0)
        )
        degree = jnp.sum(running_tally, axis=0)
        norm = 1.0 / jnp.maximum(degree, 1.0)
        scaled = (grad_out.astype(jnp.float32) * norm[:, None]).astype(jnp.bfloat16)
        return jnp.dot(
            running_tally.astype(jnp.bfloat16), scaled, preferred_element_type=jnp.float32
        ).astype(jnp.bfloat16)

    pulled = lax.map(one, (edge_dst, edge_src))
    partial_value = jnp.einsum(
        "rso,rio->si", pulled, rel_weight, preferred_element_type=jnp.float32
    )
    slot_grads = lax.psum_scatter(partial_value, "rep", scatter_dimension=1, tiled=True)
    weight_terms = jnp.einsum(
        "si,rso->rio", source_features, pulled, preferred_element_type=jnp.float32
    )
    grad_rel_weight = lax.psum(weight_terms, "dom")
    targets = target_rows.reshape(-1)
    arrived = lax.all_to_all(slot_grads, "dom", split_axis=0, concat_axis=0, tiled=True)
    owned = deliver(targets, arrived, OWN_DEV)
    self_term = jnp.einsum("do,io->di", grad_out, self_weight, preferred_element_type=jnp.float32)
    owned = owned.at[:destination_count].add(self_term)
    return (owned, grad_rel_weight)


def solution(mesh):
    in_specs = (
        P(("groups", "dom"), None),
        P(("groups", "dom"), None),
        P("rep", None, None),
        P("rep", None),
        P("rep", ("groups", "dom")),
        P("rep", ("groups", "dom")),
        P(("groups", "dom"), None),
        P(("groups", "dom"), None),
    )
    out_specs = (P(("groups", "dom"), "rep"), P(("groups", "rep"), None, None))
    return jax.shard_map(
        on_device, mesh=mesh, in_specs=in_specs, out_specs=out_specs, check_vma=False
    )
```

```python
import math

import jax
import jax.numpy as jnp
from jax import lax
from jax.experimental import pallas as pl
from jax.experimental.pallas import tpu as pltpu
from jax.sharding import PartitionSpec as P

OWN_DEV = 2048
TN = (((0,), (0,)), ((), ()))
NT = (((1,), (1,)), ((), ()))


def remap_slots(source, counts, slot_index, domain_count):
    block = source // slot_index
    position = source % slot_index
    picked = jnp.sum(
        jnp.where(block[..., None] == jnp.arange(domain_count), counts, 0), axis=-1
    )
    return block * slot_index + position % picked


def pick(first, rows, wanted):
    places = first + lax.broadcasted_iota(jnp.int32, (rows, wanted.shape[1]), 0)
    return jnp.where(places == wanted, 1.0, 0.0).astype(jnp.bfloat16)


def pull_kernel(dst_ref, slot_ref, grad_ref, pulled_ref, scaled, rows):
    destinations, width = grad_ref.shape
    edges = dst_ref.shape[1]
    tile = pulled_ref.shape[0]
    step = pl.program_id(0)

    @pl.when(step == 0)
    def _():
        block = math.gcd(destinations, 128)

        @pl.loop(0, destinations // block)
        def _(i):
            first = pl.multiple_of(i * block, block)
            places = first + lax.broadcasted_iota(jnp.int32, (block, edges), 0)
            hits = jnp.where(places == dst_ref[...], 1.0, 0.0)
            degree = jnp.sum(hits, axis=1, keepdims=True)
            norm = 1.0 / jnp.maximum(degree, 1.0)
            here = pl.ds(first, block)
            values = grad_ref[here, :].astype(jnp.float32) * norm
            scaled[:, here] = values.T.astype(jnp.bfloat16)

        chunk = math.gcd(edges, 512)

        @pl.loop(0, edges // chunk)
        def _(i):
            here = pl.ds(pl.multiple_of(i * chunk, chunk), chunk)
            picks = pick(0, destinations, dst_ref[:, here])
            rows[:, here] = jnp.dot(
                scaled[...], picks, preferred_element_type=jnp.float32
            ).astype(jnp.bfloat16)

    picks = pick(step * tile, tile, slot_ref[...])
    pulled_ref[...] = lax.dot_general(
        picks, rows[...], NT, preferred_element_type=jnp.float32
    ).astype(jnp.bfloat16)


def pull(dst, slots, grad_out, slot_count):
    destinations, width = grad_out.shape
    edges = dst.shape[1]
    tile = math.gcd(slot_count, 256)
    return pl.pallas_call(
        pull_kernel,
        grid=(slot_count // tile,),
        out_shape=jax.ShapeDtypeStruct((slot_count, width), jnp.bfloat16),
        in_specs=[
            pl.BlockSpec((1, edges), lambda i: (0, 0)),
            pl.BlockSpec((1, edges), lambda i: (0, 0)),
            pl.BlockSpec((destinations, width), lambda i: (0, 0)),
        ],
        out_specs=pl.BlockSpec((tile, width), lambda i: (i, 0)),
        scratch_shapes=[
            pltpu.VMEM((width, destinations), jnp.bfloat16),
            pltpu.VMEM((width, edges), jnp.bfloat16),
        ],
        compiler_params=pltpu.CompilerParams(vmem_limit_bytes=40 * 2**20),
        cost_estimate=pl.CostEstimate(
            flops=2 * edges * width * (destinations + slot_count),
            bytes_accessed=2 * width * (destinations + slot_count),
            transcendentals=0,
        ),
    )(dst, slots, grad_out)


def deliver_kernel(self_steps, targets_ref, arrived_ref, self_ref, owned_ref, parts):
    tile, width = owned_ref.shape
    step = pl.program_id(0)

    @pl.when(step == 0)
    def _():
        rest = arrived_ref[...]
        for i in range(3):
            part = rest.astype(jnp.bfloat16)
            parts[:, i * width : (i + 1) * width] = part
            rest = rest - part.astype(jnp.float32)

    picks = pick(step * tile, tile, targets_ref[...])
    sums = jnp.dot(picks, parts[...], preferred_element_type=jnp.float32)
    total = sums[:, 2 * width :] + sums[:, width : 2 * width] + sums[:, :width]
    owned_ref[...] = total + jnp.where(step < self_steps, self_ref[...], 0.0)


def deliver(targets, arrived, self_term, owned_rows):
    count, width = arrived.shape
    tile = math.gcd(self_term.shape[0], math.gcd(owned_rows, 512))
    self_steps = self_term.shape[0] // tile
    return pl.pallas_call(
        lambda *refs: deliver_kernel(self_steps, *refs),
        grid=(owned_rows // tile,),
        out_shape=jax.ShapeDtypeStruct((owned_rows, width), jnp.float32),
        in_specs=[
            pl.BlockSpec((1, count), lambda i: (0, 0)),
            pl.BlockSpec((count, width), lambda i: (0, 0)),
            pl.BlockSpec((tile, width), lambda i: (jnp.minimum(i, self_steps - 1), 0)),
        ],
        out_specs=pl.BlockSpec((tile, width), lambda i: (i, 0)),
        scratch_shapes=[pltpu.VMEM((count, 3 * width), jnp.bfloat16)],
        compiler_params=pltpu.CompilerParams(vmem_limit_bytes=32 * 2**20),
        cost_estimate=pl.CostEstimate(
            flops=6 * count * width * owned_rows,
            bytes_accessed=4 * width * (count + owned_rows),
            transcendentals=0,
        ),
    )(targets, arrived, self_term)


def on_device(
    grad_out, source_features, rel_weight, self_weight, edge_dst, edge_src, send_counts, target_rows
):
    domain_count = lax.axis_size("dom")
    slot_count = source_features.shape[0]
    slot_index = slot_count // domain_count
    slots = remap_slots(edge_src, send_counts[0], slot_index, domain_count)
    relations = rel_weight.shape[0]

    pulled, weight_grads = [], []
    for r in range(relations):
        here = pull(edge_dst[r : r + 1], slots[r : r + 1], grad_out, slot_count)
        terms = lax.dot_general(source_features, here, TN, preferred_element_type=jnp.float32)
        pulled.append(here)
        weight_grads.append(lax.psum(terms, "dom"))
    partial_value = sum(
        lax.dot_general(pulled[r], rel_weight[r], NT, preferred_element_type=jnp.float32)
        for r in range(relations)
    )
    slot_grads = lax.psum_scatter(partial_value, "rep", scatter_dimension=1, tiled=True)
    arrived = lax.all_to_all(slot_grads, "dom", split_axis=0, concat_axis=0, tiled=True)
    self_term = lax.dot_general(grad_out, self_weight, NT, preferred_element_type=jnp.float32)
    owned = deliver(target_rows.reshape(1, -1), arrived, self_term, OWN_DEV)
    return (owned, jnp.stack(weight_grads))


def solution(mesh):
    in_specs = (
        P(("groups", "dom"), None),
        P(("groups", "dom"), None),
        P("rep", None, None),
        P("rep", None),
        P("rep", ("groups", "dom")),
        P("rep", ("groups", "dom")),
        P(("groups", "dom"), None),
        P(("groups", "dom"), None),
    )
    out_specs = (P(("groups", "dom"), "rep"), P(("groups", "rep"), None, None))
    return jax.shard_map(
        on_device, mesh=mesh, in_specs=in_specs, out_specs=out_specs, check_vma=False
    )
```

```python
import math

import jax
import jax.numpy as jnp
from jax import lax
from jax.experimental import pallas as pl
from jax.experimental.pallas import tpu as pltpu
from jax.sharding import PartitionSpec as P

OWN_DEV = 2048
TN = (((0,), (0,)), ((), ()))
NT = (((1,), (1,)), ((), ()))


def remap_slots(source, counts, slot_index, domain_count):
    block = source // slot_index
    position = source % slot_index
    picked = jnp.sum(
        jnp.where(block[..., None] == jnp.arange(domain_count), counts, 0), axis=-1
    )
    return block * slot_index + position % picked


def pick(first, rows, wanted):
    places = first + lax.broadcasted_iota(jnp.int32, (rows, wanted.shape[1]), 0)
    return jnp.where(places == wanted, 1.0, 0.0).astype(jnp.bfloat16)


def pull_kernel(
    dst_ref, slot_ref, grad_ref, feature_ref, pulled_ref, weight_ref, scaled, rows
):
    destinations, width = grad_ref.shape
    edges = dst_ref.shape[1]
    tile = pulled_ref.shape[0]
    step = pl.program_id(0)

    @pl.when(step == 0)
    def _():
        weight_ref[...] = jnp.zeros_like(weight_ref)
        block = math.gcd(destinations, 128)

        @pl.loop(0, destinations // block)
        def _(i):
            first = pl.multiple_of(i * block, block)
            places = first + lax.broadcasted_iota(jnp.int32, (block, edges), 0)
            hits = jnp.where(places == dst_ref[...], 1.0, 0.0)
            degree = jnp.sum(hits, axis=1, keepdims=True)
            norm = 1.0 / jnp.maximum(degree, 1.0)
            here = pl.ds(first, block)
            values = grad_ref[here, :].astype(jnp.float32) * norm
            scaled[:, here] = values.T.astype(jnp.bfloat16)

        chunk = math.gcd(edges, 512)

        @pl.loop(0, edges // chunk)
        def _(i):
            here = pl.ds(pl.multiple_of(i * chunk, chunk), chunk)
            picks = pick(0, destinations, dst_ref[:, here])
            rows[:, here] = jnp.dot(
                scaled[...], picks, preferred_element_type=jnp.float32
            ).astype(jnp.bfloat16)

    picks = pick(step * tile, tile, slot_ref[...])
    pulled = lax.dot_general(
        picks, rows[...], NT, preferred_element_type=jnp.float32
    ).astype(jnp.bfloat16)
    pulled_ref[...] = pulled
    weight_ref[...] += lax.dot_general(
        feature_ref[...], pulled, TN, preferred_element_type=jnp.float32
    )


def pull(dst, slots, grad_out, features):
    destinations, width = grad_out.shape
    slot_count, inputs = features.shape
    edges = dst.shape[1]
    tile = math.gcd(slot_count, 256)
    return pl.pallas_call(
        pull_kernel,
        grid=(slot_count // tile,),
        out_shape=(
            jax.ShapeDtypeStruct((slot_count, width), jnp.bfloat16),
            jax.ShapeDtypeStruct((inputs, width), jnp.float32),
        ),
        in_specs=[
            pl.BlockSpec((1, edges), lambda i: (0, 0)),
            pl.BlockSpec((1, edges), lambda i: (0, 0)),
            pl.BlockSpec((destinations, width), lambda i: (0, 0)),
            pl.BlockSpec((tile, inputs), lambda i: (i, 0)),
        ],
        out_specs=(
            pl.BlockSpec((tile, width), lambda i: (i, 0)),
            pl.BlockSpec((inputs, width), lambda i: (0, 0)),
        ),
        scratch_shapes=[
            pltpu.VMEM((width, destinations), jnp.bfloat16),
            pltpu.VMEM((width, edges), jnp.bfloat16),
        ],
        compiler_params=pltpu.CompilerParams(vmem_limit_bytes=40 * 2**20),
        cost_estimate=pl.CostEstimate(
            flops=2 * edges * width * (destinations + slot_count),
            bytes_accessed=2 * width * (destinations + 2 * slot_count + 2 * inputs),
            transcendentals=0,
        ),
    )(dst, slots, grad_out, features)


def sum_over_line(value, axis):
    count = lax.axis_size(axis)
    if count % 2 or count > 8:
        return lax.psum(value, axis)
    me = lax.axis_index(axis)
    middle = count // 2
    for hop in range(middle - 1):
        pairs = [(hop, hop + 1), (count - 1 - hop, count - 2 - hop)]
        value = value + lax.ppermute(value, axis, pairs)
    value = value + lax.ppermute(value, axis, [(middle - 1, middle), (middle, middle - 1)])
    for hop in range(middle - 1):
        low, high = middle - 2 - hop, middle + 1 + hop
        given = lax.ppermute(value, axis, [(low + 1, low), (high - 1, high)])
        value = jnp.where((me == low) | (me == high), given, value)
    return value


def project(pulled, weights):
    return sum(
        lax.dot_general(p, w, NT, preferred_element_type=jnp.float32)
        for p, w in zip(pulled, weights)
    )


def project_and_scatter(pulled, rel_weight, axis):
    if lax.axis_size(axis) != 4:
        return lax.psum_scatter(
            project(pulled, rel_weight), axis, scatter_dimension=1, tiled=True
        )
    me = lax.axis_index(axis)
    high, low = me // 2, me % 2
    relations, inputs, outputs = rel_weight.shape
    quarters = rel_weight.reshape(relations, 2, 2, inputs // 4, outputs)

    def half(at_low):
        one = lambda at_high: lax.dynamic_slice(
            quarters,
            (0, at_high, at_low, 0, 0),
            (relations, 1, 1, inputs // 4, outputs),
        ).reshape(relations, inputs // 4, outputs)
        return jnp.concatenate([one(1 - high), one(high)], axis=1)

    sent = project(pulled, half(1 - low))
    given = lax.ppermute(sent, axis, [(i, i ^ 1) for i in range(4)])
    kept = project(pulled, half(low))
    width = inputs // 4
    crossing = kept[:, :width] + given[:, :width]
    crossed = lax.ppermute(crossing, axis, [(i, i ^ 2) for i in range(4)])
    return kept[:, width:] + given[:, width:] + crossed


def deliver_kernel(self_steps, targets_ref, arrived_ref, self_ref, owned_ref, parts):
    tile, width = owned_ref.shape
    step = pl.program_id(0)

    @pl.when(step == 0)
    def _():
        rest = arrived_ref[...]
        for i in range(3):
            part = rest.astype(jnp.bfloat16)
            parts[:, i * width : (i + 1) * width] = part
            rest = rest - part.astype(jnp.float32)

    picks = pick(step * tile, tile, targets_ref[...])
    sums = jnp.dot(picks, parts[...], preferred_element_type=jnp.float32)
    total = sums[:, 2 * width :] + sums[:, width : 2 * width] + sums[:, :width]
    owned_ref[...] = total + jnp.where(step < self_steps, self_ref[...], 0.0)


def deliver(targets, arrived, self_term, owned_rows):
    count, width = arrived.shape
    tile = math.gcd(self_term.shape[0], math.gcd(owned_rows, 512))
    self_steps = self_term.shape[0] // tile
    return pl.pallas_call(
        lambda *refs: deliver_kernel(self_steps, *refs),
        grid=(owned_rows // tile,),
        out_shape=jax.ShapeDtypeStruct((owned_rows, width), jnp.float32),
        in_specs=[
            pl.BlockSpec((1, count), lambda i: (0, 0)),
            pl.BlockSpec((count, width), lambda i: (0, 0)),
            pl.BlockSpec((tile, width), lambda i: (jnp.minimum(i, self_steps - 1), 0)),
        ],
        out_specs=pl.BlockSpec((tile, width), lambda i: (i, 0)),
        scratch_shapes=[pltpu.VMEM((count, 3 * width), jnp.bfloat16)],
        compiler_params=pltpu.CompilerParams(vmem_limit_bytes=32 * 2**20),
        cost_estimate=pl.CostEstimate(
            flops=6 * count * width * owned_rows,
            bytes_accessed=4 * width * (count + owned_rows),
            transcendentals=0,
        ),
    )(targets, arrived, self_term)


def on_device(
    grad_out, source_features, rel_weight, self_weight, edge_dst, edge_src, send_counts, target_rows
):
    domain_count = lax.axis_size("dom")
    slot_index = source_features.shape[0] // domain_count
    slots = remap_slots(edge_src, send_counts[0], slot_index, domain_count)
    relations = rel_weight.shape[0]

    pulled, weight_grads = [], []
    for r in range(relations):
        here, terms = pull(edge_dst[r : r + 1], slots[r : r + 1], grad_out, source_features)
        pulled.append(here)
        pieces = [sum_over_line(piece, "dom") for piece in jnp.split(terms, 2, axis=0)]
        weight_grads.append(jnp.concatenate(pieces, axis=0))
    slot_grads = project_and_scatter(pulled, rel_weight, "rep")
    arrived = lax.all_to_all(slot_grads, "dom", split_axis=0, concat_axis=0, tiled=True)
    self_term = lax.dot_general(grad_out, self_weight, NT, preferred_element_type=jnp.float32)
    owned = deliver(target_rows.reshape(1, -1), arrived, self_term, OWN_DEV)
    return (owned, jnp.stack(weight_grads))


def solution(mesh):
    in_specs = (
        P(("groups", "dom"), None),
        P(("groups", "dom"), None),
        P("rep", None, None),
        P("rep", None),
        P("rep", ("groups", "dom")),
        P("rep", ("groups", "dom")),
        P(("groups", "dom"), None),
        P(("groups", "dom"), None),
    )
    out_specs = (P(("groups", "dom"), "rep"), P(("groups", "rep"), None, None))
    return jax.shard_map(
        on_device, mesh=mesh, in_specs=in_specs, out_specs=out_specs, check_vma=False
    )
```

```python
import math

import jax
import jax.numpy as jnp
from jax import lax
from jax.experimental import pallas as pl
from jax.experimental.pallas import tpu as pltpu
from jax.sharding import PartitionSpec as P

OWN_DEV = 2048
TN = (((0,), (0,)), ((), ()))
NT = (((1,), (1,)), ((), ()))


def remap_slots(source, counts, slot_index, domain_count):
    block = source // slot_index
    position = source % slot_index
    picked = jnp.sum(
        jnp.where(block[..., None] == jnp.arange(domain_count), counts, 0), axis=-1
    )
    return block * slot_index + position % picked


def pick(first, rows, wanted):
    places = first + lax.broadcasted_iota(jnp.int32, (rows, wanted.shape[1]), 0)
    return jnp.where(places == wanted, 1.0, 0.0).astype(jnp.bfloat16)


def pull_kernel(
    dst_ref, slot_ref, grad_ref, feature_ref, pulled_ref, weight_ref, scaled, rows
):
    destinations, width = grad_ref.shape
    edges = dst_ref.shape[1]
    tile = pulled_ref.shape[0]
    step = pl.program_id(0)

    @pl.when(step == 0)
    def _():
        weight_ref[...] = jnp.zeros_like(weight_ref)
        block = math.gcd(destinations, 128)

        @pl.loop(0, destinations // block)
        def _(i):
            first = pl.multiple_of(i * block, block)
            places = first + lax.broadcasted_iota(jnp.int32, (block, edges), 0)
            hits = jnp.where(places == dst_ref[...], 1.0, 0.0)
            degree = jnp.sum(hits, axis=1, keepdims=True)
            norm = 1.0 / jnp.maximum(degree, 1.0)
            here = pl.ds(first, block)
            values = grad_ref[here, :].astype(jnp.float32) * norm
            scaled[:, here] = values.T.astype(jnp.bfloat16)

        chunk = math.gcd(edges, 512)

        @pl.loop(0, edges // chunk)
        def _(i):
            here = pl.ds(pl.multiple_of(i * chunk, chunk), chunk)
            picks = pick(0, destinations, dst_ref[:, here])
            rows[:, here] = jnp.dot(
                scaled[...], picks, preferred_element_type=jnp.float32
            ).astype(jnp.bfloat16)

    picks = pick(step * tile, tile, slot_ref[...])
    pulled = lax.dot_general(
        picks, rows[...], NT, preferred_element_type=jnp.float32
    ).astype(jnp.bfloat16)
    pulled_ref[...] = pulled
    weight_ref[...] += lax.dot_general(
        feature_ref[...], pulled, TN, preferred_element_type=jnp.float32
    )


def pull(dst, slots, grad_out, features):
    destinations, width = grad_out.shape
    slot_count, inputs = features.shape
    edges = dst.shape[1]
    tile = math.gcd(slot_count, 256)
    return pl.pallas_call(
        pull_kernel,
        grid=(slot_count // tile,),
        out_shape=(
            jax.ShapeDtypeStruct((slot_count, width), jnp.bfloat16),
            jax.ShapeDtypeStruct((inputs, width), jnp.float32),
        ),
        in_specs=[
            pl.BlockSpec((1, edges), lambda i: (0, 0)),
            pl.BlockSpec((1, edges), lambda i: (0, 0)),
            pl.BlockSpec((destinations, width), lambda i: (0, 0)),
            pl.BlockSpec((tile, inputs), lambda i: (i, 0)),
        ],
        out_specs=(
            pl.BlockSpec((tile, width), lambda i: (i, 0)),
            pl.BlockSpec((inputs, width), lambda i: (0, 0)),
        ),
        scratch_shapes=[
            pltpu.VMEM((width, destinations), jnp.bfloat16),
            pltpu.VMEM((width, edges), jnp.bfloat16),
        ],
        compiler_params=pltpu.CompilerParams(vmem_limit_bytes=40 * 2**20),
        cost_estimate=pl.CostEstimate(
            flops=2 * edges * width * (destinations + slot_count),
            bytes_accessed=2 * width * (destinations + 2 * slot_count + 2 * inputs),
            transcendentals=0,
        ),
    )(dst, slots, grad_out, features)


def sum_over_line(groups, axis):
    count = lax.axis_size(axis)
    if count % 2 or count > 8:
        return [lax.psum(piece, axis) for group in groups for piece in group]
    me = lax.axis_index(axis)
    middle = count // 2
    right = [(i, i + 1) for i in range(count - 1)]
    left = [(i + 1, i) for i in range(count - 1)]
    pieces = sum(len(group) for group in groups)
    held = groups[0]
    later = list(groups[1:])

    def choose(number):
        value = held[0]
        for k in range(1, len(held)):
            value = jnp.where(number >= k, held[k], value)
        return value

    for step in range(pieces + count - 2):
        if step == len(held) and later:
            held = held + later.pop(0)
        from_left = lax.ppermute(choose(step - me), axis, right)
        from_right = lax.ppermute(choose(step - (count - 1 - me)), axis, left)
        at_left, at_right = step - me + 1, step - (count - 1 - me) + 1
        new = []
        for k, value in enumerate(held):
            by_left = jnp.where(me <= middle, value + from_left, from_left)
            value = jnp.where((at_left == k) & (me > 0), by_left, value)
            by_right = jnp.where(me >= middle - 1, value + from_right, from_right)
            value = jnp.where((at_right == k) & (me < count - 1), by_right, value)
            new.append(value)
        held = new
    return held


def project(pulled, weights):
    return sum(
        lax.dot_general(p, w, NT, preferred_element_type=jnp.float32)
        for p, w in zip(pulled, weights)
    )


def project_and_scatter(pulled, rel_weight, axis):
    if lax.axis_size(axis) != 4:
        return lax.psum_scatter(
            project(pulled, rel_weight), axis, scatter_dimension=1, tiled=True
        )
    me = lax.axis_index(axis)
    high, low = me // 2, me % 2
    relations, inputs, outputs = rel_weight.shape
    quarters = rel_weight.reshape(relations, 2, 2, inputs // 4, outputs)

    def half(at_low):
        one = lambda at_high: lax.dynamic_slice(
            quarters,
            (0, at_high, at_low, 0, 0),
            (relations, 1, 1, inputs // 4, outputs),
        ).reshape(relations, inputs // 4, outputs)
        return jnp.concatenate([one(1 - high), one(high)], axis=1)

    sent = project(pulled, half(1 - low))
    given = lax.ppermute(sent, axis, [(i, i ^ 1) for i in range(4)])
    kept = project(pulled, half(low))
    width = inputs // 4
    crossing = kept[:, :width] + given[:, :width]
    crossed = lax.ppermute(crossing, axis, [(i, i ^ 2) for i in range(4)])
    return kept[:, width:] + given[:, width:] + crossed


def deliver_kernel(self_steps, targets_ref, arrived_ref, self_ref, owned_ref, parts):
    tile, width = owned_ref.shape
    step = pl.program_id(0)

    @pl.when(step == 0)
    def _():
        rest = arrived_ref[...]
        for i in range(3):
            part = rest.astype(jnp.bfloat16)
            parts[:, i * width : (i + 1) * width] = part
            rest = rest - part.astype(jnp.float32)

    picks = pick(step * tile, tile, targets_ref[...])
    sums = jnp.dot(picks, parts[...], preferred_element_type=jnp.float32)
    total = sums[:, 2 * width :] + sums[:, width : 2 * width] + sums[:, :width]
    owned_ref[...] = total + jnp.where(step < self_steps, self_ref[...], 0.0)


def deliver(targets, arrived, self_term, owned_rows):
    count, width = arrived.shape
    tile = math.gcd(self_term.shape[0], math.gcd(owned_rows, 512))
    self_steps = self_term.shape[0] // tile
    return pl.pallas_call(
        lambda *refs: deliver_kernel(self_steps, *refs),
        grid=(owned_rows // tile,),
        out_shape=jax.ShapeDtypeStruct((owned_rows, width), jnp.float32),
        in_specs=[
            pl.BlockSpec((1, count), lambda i: (0, 0)),
            pl.BlockSpec((count, width), lambda i: (0, 0)),
            pl.BlockSpec((tile, width), lambda i: (jnp.minimum(i, self_steps - 1), 0)),
        ],
        out_specs=pl.BlockSpec((tile, width), lambda i: (i, 0)),
        scratch_shapes=[pltpu.VMEM((count, 3 * width), jnp.bfloat16)],
        compiler_params=pltpu.CompilerParams(vmem_limit_bytes=32 * 2**20),
        cost_estimate=pl.CostEstimate(
            flops=6 * count * width * owned_rows,
            bytes_accessed=4 * width * (count + owned_rows),
            transcendentals=0,
        ),
    )(targets, arrived, self_term)


def on_device(
    grad_out, source_features, rel_weight, self_weight, edge_dst, edge_src, send_counts, target_rows
):
    domain_count = lax.axis_size("dom")
    slot_index = source_features.shape[0] // domain_count
    slots = remap_slots(edge_src, send_counts[0], slot_index, domain_count)
    relations = rel_weight.shape[0]

    pulled, groups = [], []
    for r in range(relations):
        here, terms = pull(edge_dst[r : r + 1], slots[r : r + 1], grad_out, source_features)
        pulled.append(here)
        groups.append(list(jnp.split(terms, 2, axis=0)))
    pieces = sum_over_line(groups, "dom")
    weight_grads = jnp.concatenate(pieces, axis=0).reshape(rel_weight.shape)
    slot_grads = project_and_scatter(pulled, rel_weight, "rep")
    arrived = lax.all_to_all(slot_grads, "dom", split_axis=0, concat_axis=0, tiled=True)
    self_term = lax.dot_general(grad_out, self_weight, NT, preferred_element_type=jnp.float32)
    owned = deliver(target_rows.reshape(1, -1), arrived, self_term, OWN_DEV)
    return (owned, weight_grads)


def solution(mesh):
    in_specs = (
        P(("groups", "dom"), None),
        P(("groups", "dom"), None),
        P("rep", None, None),
        P("rep", None),
        P("rep", ("groups", "dom")),
        P("rep", ("groups", "dom")),
        P(("groups", "dom"), None),
        P(("groups", "dom"), None),
    )
    out_specs = (P(("groups", "dom"), "rep"), P(("groups", "rep"), None, None))
    return jax.shard_map(
        on_device, mesh=mesh, in_specs=in_specs, out_specs=out_specs, check_vma=False
    )
```

```python
import math

import jax
import jax.numpy as jnp
from jax import lax
from jax.experimental import pallas as pl
from jax.experimental.pallas import tpu as pltpu
from jax.sharding import PartitionSpec as P

OWN_DEV = 2048
TN = (((0,), (0,)), ((), ()))
NT = (((1,), (1,)), ((), ()))


def remap_slots(source, counts, slot_index, domain_count):
    block = source // slot_index
    position = source % slot_index
    picked = jnp.sum(
        jnp.where(block[..., None] == jnp.arange(domain_count), counts, 0), axis=-1
    )
    return block * slot_index + position % picked


def pick(first, rows, wanted):
    places = first + lax.broadcasted_iota(jnp.int32, (rows, wanted.shape[1]), 0)
    return jnp.where(places == wanted, 1.0, 0.0).astype(jnp.bfloat16)


def pull_kernel(
    dst_ref, slot_ref, grad_ref, feature_ref, pulled_ref, weight_ref, scaled, rows
):
    destinations, width = grad_ref.shape
    edges = dst_ref.shape[1]
    tile = pulled_ref.shape[0]
    step = pl.program_id(0)

    @pl.when(step == 0)
    def _():
        weight_ref[...] = jnp.zeros_like(weight_ref)
        block = math.gcd(destinations, 128)

        @pl.loop(0, destinations // block)
        def _(i):
            first = pl.multiple_of(i * block, block)
            places = first + lax.broadcasted_iota(jnp.int32, (block, edges), 0)
            hits = jnp.where(places == dst_ref[...], 1.0, 0.0)
            degree = jnp.sum(hits, axis=1, keepdims=True)
            norm = 1.0 / jnp.maximum(degree, 1.0)
            here = pl.ds(first, block)
            values = grad_ref[here, :].astype(jnp.float32) * norm
            scaled[:, here] = values.T.astype(jnp.bfloat16)

        chunk = math.gcd(edges, 512)

        @pl.loop(0, edges // chunk)
        def _(i):
            here = pl.ds(pl.multiple_of(i * chunk, chunk), chunk)
            picks = pick(0, destinations, dst_ref[:, here])
            rows[:, here] = jnp.dot(
                scaled[...], picks, preferred_element_type=jnp.float32
            ).astype(jnp.bfloat16)

    picks = pick(step * tile, tile, slot_ref[...])
    pulled = lax.dot_general(
        picks, rows[...], NT, preferred_element_type=jnp.float32
    ).astype(jnp.bfloat16)
    pulled_ref[...] = pulled
    weight_ref[...] += lax.dot_general(
        feature_ref[...], pulled, TN, preferred_element_type=jnp.float32
    )


def pull(dst, slots, grad_out, features):
    destinations, width = grad_out.shape
    slot_count, inputs = features.shape
    edges = dst.shape[1]
    tile = math.gcd(slot_count, 256)
    return pl.pallas_call(
        pull_kernel,
        grid=(slot_count // tile,),
        out_shape=(
            jax.ShapeDtypeStruct((slot_count, width), jnp.bfloat16),
            jax.ShapeDtypeStruct((inputs, width), jnp.float32),
        ),
        in_specs=[
            pl.BlockSpec((1, edges), lambda i: (0, 0)),
            pl.BlockSpec((1, edges), lambda i: (0, 0)),
            pl.BlockSpec((destinations, width), lambda i: (0, 0)),
            pl.BlockSpec((tile, inputs), lambda i: (i, 0)),
        ],
        out_specs=(
            pl.BlockSpec((tile, width), lambda i: (i, 0)),
            pl.BlockSpec((inputs, width), lambda i: (0, 0)),
        ),
        scratch_shapes=[
            pltpu.VMEM((width, destinations), jnp.bfloat16),
            pltpu.VMEM((width, edges), jnp.bfloat16),
        ],
        compiler_params=pltpu.CompilerParams(vmem_limit_bytes=40 * 2**20),
        cost_estimate=pl.CostEstimate(
            flops=2 * edges * width * (destinations + slot_count),
            bytes_accessed=2 * width * (destinations + 2 * slot_count + 2 * inputs),
            transcendentals=0,
        ),
    )(dst, slots, grad_out, features)


def sum_over(value, axis, in_two):
    if in_two and value.shape[0] % lax.axis_size(axis) == 0:
        share = lax.psum_scatter(value, axis, scatter_dimension=0, tiled=True)
        return lax.all_gather(share, axis, axis=0, tiled=True)
    return lax.psum(value, axis)


def project(pulled, weights):
    return sum(
        lax.dot_general(p, w, NT, preferred_element_type=jnp.float32)
        for p, w in zip(pulled, weights)
    )


def project_and_scatter(pulled, rel_weight, axis):
    if lax.axis_size(axis) != 4:
        return lax.psum_scatter(
            project(pulled, rel_weight), axis, scatter_dimension=1, tiled=True
        )
    me = lax.axis_index(axis)
    high, low = me // 2, me % 2
    relations, inputs, outputs = rel_weight.shape
    quarters = rel_weight.reshape(relations, 2, 2, inputs // 4, outputs)

    def half(at_low):
        one = lambda at_high: lax.dynamic_slice(
            quarters,
            (0, at_high, at_low, 0, 0),
            (relations, 1, 1, inputs // 4, outputs),
        ).reshape(relations, inputs // 4, outputs)
        return jnp.concatenate([one(1 - high), one(high)], axis=1)

    sent = project(pulled, half(1 - low))
    given = lax.ppermute(sent, axis, [(i, i ^ 1) for i in range(4)])
    kept = project(pulled, half(low))
    width = inputs // 4
    crossing = kept[:, :width] + given[:, :width]
    crossed = lax.ppermute(crossing, axis, [(i, i ^ 2) for i in range(4)])
    return kept[:, width:] + given[:, width:] + crossed


def deliver_kernel(self_steps, targets_ref, arrived_ref, self_ref, owned_ref, parts):
    tile, width = owned_ref.shape
    step = pl.program_id(0)

    @pl.when(step == 0)
    def _():
        rest = arrived_ref[...]
        for i in range(3):
            part = rest.astype(jnp.bfloat16)
            parts[:, i * width : (i + 1) * width] = part
            rest = rest - part.astype(jnp.float32)

    picks = pick(step * tile, tile, targets_ref[...])
    sums = jnp.dot(picks, parts[...], preferred_element_type=jnp.float32)
    total = sums[:, 2 * width :] + sums[:, width : 2 * width] + sums[:, :width]
    owned_ref[...] = total + jnp.where(step < self_steps, self_ref[...], 0.0)


def deliver(targets, arrived, self_term, owned_rows):
    count, width = arrived.shape
    tile = math.gcd(self_term.shape[0], math.gcd(owned_rows, 512))
    self_steps = self_term.shape[0] // tile
    return pl.pallas_call(
        lambda *refs: deliver_kernel(self_steps, *refs),
        grid=(owned_rows // tile,),
        out_shape=jax.ShapeDtypeStruct((owned_rows, width), jnp.float32),
        in_specs=[
            pl.BlockSpec((1, count), lambda i: (0, 0)),
            pl.BlockSpec((count, width), lambda i: (0, 0)),
            pl.BlockSpec((tile, width), lambda i: (jnp.minimum(i, self_steps - 1), 0)),
        ],
        out_specs=pl.BlockSpec((tile, width), lambda i: (i, 0)),
        scratch_shapes=[pltpu.VMEM((count, 3 * width), jnp.bfloat16)],
        compiler_params=pltpu.CompilerParams(vmem_limit_bytes=32 * 2**20),
        cost_estimate=pl.CostEstimate(
            flops=6 * count * width * owned_rows,
            bytes_accessed=4 * width * (count + owned_rows),
            transcendentals=0,
        ),
    )(targets, arrived, self_term)


def on_device(
    grad_out, source_features, rel_weight, self_weight, edge_dst, edge_src, send_counts, target_rows
):
    domain_count = lax.axis_size("dom")
    slot_index = source_features.shape[0] // domain_count
    slots = remap_slots(edge_src, send_counts[0], slot_index, domain_count)
    relations = rel_weight.shape[0]

    pulled, weight_grads = [], []
    for r in range(relations):
        here, terms = pull(edge_dst[r : r + 1], slots[r : r + 1], grad_out, source_features)
        pulled.append(here)
        weight_grads.append(sum_over(terms, "dom", r % 2 == 0))
    slot_grads = project_and_scatter(pulled, rel_weight, "rep")
    arrived = lax.all_to_all(slot_grads, "dom", split_axis=0, concat_axis=0, tiled=True)
    self_term = lax.dot_general(grad_out, self_weight, NT, preferred_element_type=jnp.float32)
    owned = deliver(target_rows.reshape(1, -1), arrived, self_term, OWN_DEV)
    return (owned, jnp.stack(weight_grads))


def solution(mesh):
    in_specs = (
        P(("groups", "dom"), None),
        P(("groups", "dom"), None),
        P("rep", None, None),
        P("rep", None),
        P("rep", ("groups", "dom")),
        P("rep", ("groups", "dom")),
        P(("groups", "dom"), None),
        P(("groups", "dom"), None),
    )
    out_specs = (P(("groups", "dom"), "rep"), P(("groups", "rep"), None, None))
    return jax.shard_map(
        on_device, mesh=mesh, in_specs=in_specs, out_specs=out_specs, check_vma=False
    )
```

```python
import math

import jax
import jax.numpy as jnp
from jax import lax
from jax.experimental import pallas as pl
from jax.experimental.pallas import tpu as pltpu
from jax.sharding import PartitionSpec as P

OWN_DEV = 2048
TN = (((0,), (0,)), ((), ()))
NT = (((1,), (1,)), ((), ()))


def remap_slots(source, counts, slot_index, domain_count):
    block = source // slot_index
    position = source % slot_index
    picked = jnp.sum(
        jnp.where(block[..., None] == jnp.arange(domain_count), counts, 0), axis=-1
    )
    return block * slot_index + position % picked


def pick(first, rows, wanted):
    places = first + lax.broadcasted_iota(jnp.int32, (rows, wanted.shape[1]), 0)
    return jnp.where(places == wanted, 1.0, 0.0).astype(jnp.bfloat16)


def pull_kernel(
    dst_ref, slot_ref, grad_ref, feature_ref, pulled_ref, weight_ref, scaled, rows
):
    destinations, width = grad_ref.shape
    edges = dst_ref.shape[1]
    tile = pulled_ref.shape[0]
    step = pl.program_id(0)

    @pl.when(step == 0)
    def _():
        weight_ref[...] = jnp.zeros_like(weight_ref)
        block = math.gcd(destinations, 128)

        @pl.loop(0, destinations // block)
        def _(i):
            first = pl.multiple_of(i * block, block)
            places = first + lax.broadcasted_iota(jnp.int32, (block, edges), 0)
            hits = jnp.where(places == dst_ref[...], 1.0, 0.0)
            degree = jnp.sum(hits, axis=1, keepdims=True)
            norm = 1.0 / jnp.maximum(degree, 1.0)
            here = pl.ds(first, block)
            values = grad_ref[here, :].astype(jnp.float32) * norm
            scaled[:, here] = values.T.astype(jnp.bfloat16)

        chunk = math.gcd(edges, 512)

        @pl.loop(0, edges // chunk)
        def _(i):
            here = pl.ds(pl.multiple_of(i * chunk, chunk), chunk)
            picks = pick(0, destinations, dst_ref[:, here])
            rows[:, here] = jnp.dot(
                scaled[...], picks, preferred_element_type=jnp.float32
            ).astype(jnp.bfloat16)

    picks = pick(step * tile, tile, slot_ref[...])
    pulled = lax.dot_general(
        picks, rows[...], NT, preferred_element_type=jnp.float32
    ).astype(jnp.bfloat16)
    pulled_ref[...] = pulled
    weight_ref[...] += lax.dot_general(
        feature_ref[...], pulled, TN, preferred_element_type=jnp.float32
    )


def pull(dst, slots, grad_out, features):
    destinations, width = grad_out.shape
    slot_count, inputs = features.shape
    edges = dst.shape[1]
    tile = math.gcd(slot_count, 256)
    return pl.pallas_call(
        pull_kernel,
        grid=(slot_count // tile,),
        out_shape=(
            jax.ShapeDtypeStruct((slot_count, width), jnp.bfloat16),
            jax.ShapeDtypeStruct((inputs, width), jnp.float32),
        ),
        in_specs=[
            pl.BlockSpec((1, edges), lambda i: (0, 0)),
            pl.BlockSpec((1, edges), lambda i: (0, 0)),
            pl.BlockSpec((destinations, width), lambda i: (0, 0)),
            pl.BlockSpec((tile, inputs), lambda i: (i, 0)),
        ],
        out_specs=(
            pl.BlockSpec((tile, width), lambda i: (i, 0)),
            pl.BlockSpec((inputs, width), lambda i: (0, 0)),
        ),
        scratch_shapes=[
            pltpu.VMEM((width, destinations), jnp.bfloat16),
            pltpu.VMEM((width, edges), jnp.bfloat16),
        ],
        compiler_params=pltpu.CompilerParams(vmem_limit_bytes=40 * 2**20),
        cost_estimate=pl.CostEstimate(
            flops=2 * edges * width * (destinations + slot_count),
            bytes_accessed=2 * width * (destinations + 2 * slot_count + 2 * inputs),
            transcendentals=0,
        ),
    )(dst, slots, grad_out, features)


def sum_over(value, axis, dimension):
    if value.shape[dimension] % (128 * lax.axis_size(axis)):
        return lax.psum(value, axis)
    share = lax.psum_scatter(value, axis, scatter_dimension=dimension, tiled=True)
    return lax.all_gather(share, axis, axis=dimension, tiled=True)


def project(pulled, weights):
    return sum(
        lax.dot_general(p, w, NT, preferred_element_type=jnp.float32)
        for p, w in zip(pulled, weights)
    )


def project_and_scatter(pulled, rel_weight, axis):
    if lax.axis_size(axis) != 4:
        return lax.psum_scatter(
            project(pulled, rel_weight), axis, scatter_dimension=1, tiled=True
        )
    me = lax.axis_index(axis)
    high, low = me // 2, me % 2
    relations, inputs, outputs = rel_weight.shape
    quarters = rel_weight.reshape(relations, 2, 2, inputs // 4, outputs)

    def half(at_low):
        one = lambda at_high: lax.dynamic_slice(
            quarters,
            (0, at_high, at_low, 0, 0),
            (relations, 1, 1, inputs // 4, outputs),
        ).reshape(relations, inputs // 4, outputs)
        return jnp.concatenate([one(1 - high), one(high)], axis=1)

    sent = project(pulled, half(1 - low))
    given = lax.ppermute(sent, axis, [(i, i ^ 1) for i in range(4)])
    kept = project(pulled, half(low))
    width = inputs // 4
    crossing = kept[:, :width] + given[:, :width]
    crossed = lax.ppermute(crossing, axis, [(i, i ^ 2) for i in range(4)])
    return kept[:, width:] + given[:, width:] + crossed


def deliver_kernel(self_steps, targets_ref, arrived_ref, self_ref, owned_ref, parts):
    tile, width = owned_ref.shape
    step = pl.program_id(0)

    @pl.when(step == 0)
    def _():
        rest = arrived_ref[...]
        for i in range(3):
            part = rest.astype(jnp.bfloat16)
            parts[:, i * width : (i + 1) * width] = part
            rest = rest - part.astype(jnp.float32)

    picks = pick(step * tile, tile, targets_ref[...])
    sums = jnp.dot(picks, parts[...], preferred_element_type=jnp.float32)
    total = sums[:, 2 * width :] + sums[:, width : 2 * width] + sums[:, :width]
    owned_ref[...] = total + jnp.where(step < self_steps, self_ref[...], 0.0)


def deliver(targets, arrived, self_term, owned_rows):
    count, width = arrived.shape
    tile = math.gcd(self_term.shape[0], math.gcd(owned_rows, 512))
    self_steps = self_term.shape[0] // tile
    return pl.pallas_call(
        lambda *refs: deliver_kernel(self_steps, *refs),
        grid=(owned_rows // tile,),
        out_shape=jax.ShapeDtypeStruct((owned_rows, width), jnp.float32),
        in_specs=[
            pl.BlockSpec((1, count), lambda i: (0, 0)),
            pl.BlockSpec((count, width), lambda i: (0, 0)),
            pl.BlockSpec((tile, width), lambda i: (jnp.minimum(i, self_steps - 1), 0)),
        ],
        out_specs=pl.BlockSpec((tile, width), lambda i: (i, 0)),
        scratch_shapes=[pltpu.VMEM((count, 3 * width), jnp.bfloat16)],
        compiler_params=pltpu.CompilerParams(vmem_limit_bytes=32 * 2**20),
        cost_estimate=pl.CostEstimate(
            flops=6 * count * width * owned_rows,
            bytes_accessed=4 * width * (count + owned_rows),
            transcendentals=0,
        ),
    )(targets, arrived, self_term)


def on_device(
    grad_out, source_features, rel_weight, self_weight, edge_dst, edge_src, send_counts, target_rows
):
    domain_count = lax.axis_size("dom")
    slot_index = source_features.shape[0] // domain_count
    slots = remap_slots(edge_src, send_counts[0], slot_index, domain_count)
    relations = rel_weight.shape[0]

    pulled, weight_grads = [], []
    for r in range(relations):
        here, terms = pull(edge_dst[r : r + 1], slots[r : r + 1], grad_out, source_features)
        pulled.append(here)
        weight_grads.append(sum_over(terms, "dom", r % 2))
    slot_grads = project_and_scatter(pulled, rel_weight, "rep")
    arrived = lax.all_to_all(slot_grads, "dom", split_axis=0, concat_axis=0, tiled=True)
    self_term = lax.dot_general(grad_out, self_weight, NT, preferred_element_type=jnp.float32)
    owned = deliver(target_rows.reshape(1, -1), arrived, self_term, OWN_DEV)
    return (owned, jnp.stack(weight_grads))


def solution(mesh):
    in_specs = (
        P(("groups", "dom"), None),
        P(("groups", "dom"), None),
        P("rep", None, None),
        P("rep", None),
        P("rep", ("groups", "dom")),
        P("rep", ("groups", "dom")),
        P(("groups", "dom"), None),
        P(("groups", "dom"), None),
    )
    out_specs = (P(("groups", "dom"), "rep"), P(("groups", "rep"), None, None))
    return jax.shard_map(
        on_device, mesh=mesh, in_specs=in_specs, out_specs=out_specs, check_vma=False
    )
```
